32 devices in a mesh: blk: 16 (over z, x, core), rep: 2 (over y).
Axes of the slice: x: 2, y: 2, z: 4, core: 2. Of those that a mesh axis runs over, the one named last changes fastest.
Arguments:
- users: float32 [32768, 256], P(('blk', 'rep')), may hold values from -1 to 1
- items: bfloat16 [32768, 256], P(('blk', 'rep')), may hold values from -1 to 1
- hot_factors: float32 [512, 256], P('rep'), may hold values from -1 to 1
- slot_items: int32 [4, 16, 32768], P(None, None, ('blk', 'rep')), may hold values from 0 to 1023
- slot_values: bfloat16 [4, 16, 32768], P(None, None, ('blk', 'rep')), may hold values from -5 to 5
- slot_lengths: int32 [4, 32768], P(None, ('blk', 'rep')), may hold values from 1 to 16
- hot_ids: int32 [8192], P(('blk', 'rep')), may hold values from 0 to 511
- hot_count: int32 [32], P(('blk', 'rep')), may hold values from 128 to 256
- hot_values: bfloat16 [32768, 256], P(('blk', 'rep')), may hold values from -5 to 5
- hot_lengths: int32 [32768], P(('blk', 'rep')), may hold values from 0 to 256
Outputs:
- new_users: float32 [32768, 256], P(('blk', 'rep'))
- new_items: bfloat16 [32768, 256], P(('blk', 'rep'))
- new_hot: float32 [512, 256], P('rep')
The draws below stay inside these ranges and needn't reach their ends.
Inputs may be any that keep to these rules, and one draw needn't show every extreme that they name: `hot_ids`: ids may repeat within a device.
All inputs are finite; a program needn't handle non-finite values.
Results may differ from the reference program's by a relative error of at most 0.0015.
The reference program's roundings to bfloat16 on the way (of `hot_slot_bf`, `hot_err_bf`, `err_bf` and `block`) count: a program that leaves them out, or rounds other values in their place, can miss the bound.
Values may be sent and summed in bfloat16 or wider, within the bound.
A program may use at most 64 MiB of HBM per device.

```python
import math
import jax
import jax.numpy as jnp
import numpy as np
from jax import lax

K = 256
U_DEV = 1024
I_BLK = 1024
P_SIZE = 16
HOT = 512
HOT_SLOTS = 256
STOPS = 4
DEVS = 32
USERS = 32768
ITEMS = 32768
N_BLK = 16
N_REP = 2


def drawn_rows(key, rows, width, scale):
    return scale * jax.random.truncated_normal(key, -4.0, 4.0, (rows, width), jnp.float32)


def draw_users(key, part):
    key = jax.random.fold_in(key, 21)
    return drawn_rows(key, USERS, K, 0.25)


def draw_items(key, part):
    key = jax.random.fold_in(key, 22)
    return drawn_rows(key, ITEMS, K, 0.25).astype(jnp.bfloat16)


def draw_hot_factors(key, part):
    key = jax.random.fold_in(key, 23)
    return drawn_rows(key, HOT, K, 0.25)


def draw_hot_count(key, part):
    first = jax.random.fold_in(key, 11)
    second = jax.random.fold_in(key, 12)
    third = jax.random.fold_in(key, 13)
    counts = jax.random.randint(first, (DEVS,), HOT_SLOTS // 2, HOT_SLOTS + 1)
    top_place = jax.random.randint(second, (), 0, DEVS)
    low_place = (top_place + jax.random.randint(third, (), 1, DEVS)) % DEVS
    places = lax.broadcasted_iota(jnp.int32, (DEVS,), 0)
    counts = jnp.where(places == top_place, HOT_SLOTS, counts)
    counts = jnp.where(places == low_place, HOT_SLOTS // 2, counts)
    return counts.astype(jnp.int32)


def place_ends(values, own_key, least, high):
    shape = values.shape
    index_at = [jax.random.randint(jax.random.fold_in(own_key, axis), (), 0, shape[axis]) for axis in range(len(shape))]
    values = values.at[tuple(index_at)].set(least)
    longest = shape.index(max(shape))
    index_at[longest] = (index_at[longest] + 1) % shape[longest]
    return values.at[tuple(index_at)].set(high)


def shard_levels(own_key, extent, shards, smallest, top_value):
    level, own = 1.0, jax.random.fold_in(own_key, 6)
    for axis_at, blocks in shards:
        steps = jnp.exp(jax.random.uniform(jax.random.fold_in(own, axis_at), (blocks,), jnp.float32, smallest / len(shards), top_value / len(shards)))
        level = level * jnp.repeat(steps, extent[axis_at] // blocks).reshape([-1 if axis == axis_at else 1 for axis in range(len(extent))])
    return level


def rank_bounds(number_of, slope):
    portions = [(1 << 20) // math.isqrt(standing ** slope) + 1 for standing in range(1, number_of + 1)]
    deviation = 1 + sum(portions) // (1 << 30)
    return np.cumsum(np.array([max(1, weight // deviation) for weight in portions]))


def skewed_ids(rng, shape, count, slope):
    grid = rank_bounds(count, slope)
    pick = jax.random.randint(jax.random.fold_in(rng, 1), shape, 0, int(grid[count - 1]))
    rank = jnp.searchsorted(jnp.asarray(grid, jnp.int32), pick, side="right")
    return jax.random.permutation(jax.random.fold_in(rng, 2), count)[rank].astype(jnp.int32)


def gaussian(stream_key, shape, scale, reach, split=(), held_as=jnp.bfloat16):
    values = jax.random.normal(stream_key, shape, jnp.float32) * scale
    if len(split) > 0:
        values = shard_levels(stream_key, shape, split, -0.22, 0.18) * values
    return jnp.clip(values, min=-reach, max=reach).astype(held_as)


def setup_inputs(seed: int = 0) -> dict:
    splits = jax.random.split(jax.random.key(seed), 11)
    users = draw_users(jax.random.fold_in(splits[10], 71), 0)
    items = draw_items(jax.random.fold_in(splits[10], 71), 0)
    hot_factors = draw_hot_factors(jax.random.fold_in(splits[10], 71), 0)
    slot_items = place_ends(jax.random.randint(splits[3], (STOPS, P_SIZE, USERS), 0, I_BLK), jax.random.fold_in(splits[3], 1), 0, I_BLK - 1).astype(jnp.int32)
    slot_values = gaussian(splits[4], (STOPS, P_SIZE, USERS), 1.0, 5.0, ((2, 32),))
    slot_lengths = place_ends(jax.random.randint(splits[5], (STOPS, USERS), 1, P_SIZE + 1), jax.random.fold_in(splits[5], 1), 1, P_SIZE).astype(jnp.int32)
    hot_ids = place_ends(skewed_ids(splits[6], (DEVS * HOT_SLOTS,), HOT, 1), jax.random.fold_in(splits[6], 3), 0, HOT - 1).astype(jnp.int32)
    hot_count = draw_hot_count(jax.random.fold_in(splits[10], 71), 0)
    hot_values = gaussian(splits[8], (USERS, HOT_SLOTS), 1.0, 5.0, ((0, 32),))
    hot_lengths = place_ends(jax.random.randint(splits[9], (USERS,), 0, HOT_SLOTS + 1), jax.random.fold_in(splits[9], 1), 0, HOT_SLOTS).astype(jnp.int32)
    return {"users": users, "items": items, "hot_factors": hot_factors, "slot_items": slot_items, "slot_values": slot_values, "slot_lengths": slot_lengths, "hot_ids": hot_ids, "hot_count": hot_count, "hot_values": hot_values, "hot_lengths": hot_lengths}


LEARN_RATE = 0.03
DECAY_RATE = 0.02
LEARN_HOT = 0.005
HOT_USER_SCALE = 1.6


def build_block(slot_items, slot_values, slot_lengths, width):
    columns = lax.broadcasted_iota(jnp.int32, (slot_items.shape[1], width), 1)
    rating_sum = jnp.zeros((slot_items.shape[1], width), jnp.float32)
    rating_count = jnp.zeros((slot_items.shape[1], width), jnp.float32)
    for position in range(slot_items.shape[0]):
        slot_hit = (slot_items[position][:, None] == columns) & (position < slot_lengths)[:, None]
        rating_sum = rating_sum + jnp.where(slot_hit, slot_values[position].astype(jnp.float32)[:, None], jnp.float32(0.0))
        rating_count = rating_count + slot_hit.astype(jnp.float32)
    return rating_sum, rating_count


def stop_update(user_rows, block, slot_items, slot_values, slot_lengths):
    user_bf = user_rows.astype(jnp.bfloat16)
    predicted = jnp.dot(user_bf, block.T, preferred_element_type=jnp.float32)
    rating_sum, rating_count = build_block(slot_items, slot_values, slot_lengths, block.shape[0])
    err_bf = (rating_sum - rating_count * predicted).astype(jnp.bfloat16)
    grad_users = jnp.dot(err_bf, block, preferred_element_type=jnp.float32)
    grad_items = jnp.dot(err_bf.T, user_bf, preferred_element_type=jnp.float32)
    block_float = block.astype(jnp.float32)
    new_rows = user_rows + LEARN_RATE * (grad_users - DECAY_RATE * user_rows)
    new_block = (block_float + LEARN_RATE * (grad_items - DECAY_RATE * block_float)).astype(jnp.bfloat16)
    return new_rows, new_block


def hot_terms(user_rows, hot_full, slot_ids, live_count, hot_values, hot_lengths):
    selector = (slot_ids[:, None] == lax.broadcasted_iota(jnp.int32, (slot_ids.shape[0], hot_full.shape[0]), 1)).astype(jnp.float32)
    hot_slot_bf = jnp.dot(selector, hot_full, precision=lax.Precision.HIGHEST).astype(jnp.bfloat16)
    user_bf = user_rows.astype(jnp.bfloat16)
    hot_predicted = jnp.dot(user_bf, hot_slot_bf.T, preferred_element_type=jnp.float32)
    positions = lax.broadcasted_iota(jnp.int32, hot_values.shape, 1)
    valid = positions < jnp.minimum(hot_lengths, live_count[0])[:, None]
    hot_err_bf = jnp.where(valid, hot_values.astype(jnp.float32) - hot_predicted, jnp.float32(0.0)).astype(jnp.bfloat16)
    slot_grads = jnp.dot(hot_err_bf.T, user_bf, preferred_element_type=jnp.float32)
    grad_dense = jnp.dot(selector.T, slot_grads, precision=lax.Precision.HIGHEST)
    pulled = jnp.dot(hot_err_bf, hot_slot_bf, preferred_element_type=jnp.float32)
    user_rate = HOT_USER_SCALE / hot_values.shape[1]
    new_rows = user_rows + user_rate * (pulled - DECAY_RATE * user_rows)
    return new_rows, grad_dense


def reference(users, items, hot_factors, slot_items, slot_values, slot_lengths, hot_ids, hot_count, hot_values, hot_lengths):
    device_count = N_BLK * N_REP
    user_blocks = users.reshape(device_count, U_DEV, K)
    slot_table = hot_ids.reshape(device_count, HOT_SLOTS)
    live_table = hot_count.reshape(device_count, 1)
    hot_value_blocks = hot_values.reshape(device_count, U_DEV, HOT_SLOTS)
    hot_length_blocks = hot_lengths.reshape(device_count, U_DEV)

    def hot_device(packed):
        return hot_terms(packed[0], hot_factors, packed[1], packed[2], packed[3], packed[4])

    user_blocks, grads = lax.map(hot_device, (user_blocks, slot_table, live_table, hot_value_blocks, hot_length_blocks))
    grad_sum = jnp.sum(grads, axis=0)
    new_hot = hot_factors + LEARN_HOT * (grad_sum - DECAY_RATE * hot_factors)
    item_blocks = items.reshape(device_count, I_BLK, K)
    item_slots = slot_items.reshape(STOPS, P_SIZE, device_count, U_DEV)
    value_slots = slot_values.reshape(STOPS, P_SIZE, device_count, U_DEV)
    length_slots = slot_lengths.reshape(STOPS, device_count, U_DEV)

    def stop_device(packed):
        return stop_update(packed[0], packed[1], packed[2], packed[3], packed[4])

    for stop_index in range(STOPS):
        user_blocks, item_blocks = lax.map(stop_device, (user_blocks, item_blocks, jnp.transpose(item_slots[stop_index], (1, 0, 2)), jnp.transpose(value_slots[stop_index], (1, 0, 2)), length_slots[stop_index]))
        item_blocks = jnp.roll(item_blocks, 1, axis=0)
    return user_blocks.reshape(USERS, K), item_blocks.reshape(ITEMS, K), new_hot
```

```python
import functools

import jax
import jax.numpy as jnp
from jax import lax
from jax.experimental import pallas as pl
from jax.experimental.pallas import tpu as pltpu
from jax.sharding import PartitionSpec as P

LEARN_RATE = 0.03
DECAY_RATE = 0.02
LEARN_HOT = 0.005
HOT_USER_SCALE = 1.6

F32 = jnp.float32
BF16 = jnp.bfloat16
MESH = pl.DeviceIdType.MESH
GROUP = 16
LO = 128
CHUNK = 256


def nn(a, b):
    return lax.dot_general(a, b, (((1,), (0,)), ((), ())), preferred_element_type=F32)


def nt(a, b):
    return lax.dot_general(a, b, (((1,), (1,)), ((), ())), preferred_element_type=F32)


def iota(shape, dim):
    return lax.broadcasted_iota(jnp.int32, shape, dim)


def one_hot(mask):
    return jnp.where(mask, 1.0, 0.0).astype(F32)


def reduce_plan(n_blk, rows):
    plan, held, bit = [], rows, 1
    while bit < n_blk:
        halve = held >= 32
        plan.append((bit, held, halve))
        held = held // 2 if halve else held
        bit *= 2
    return plan, held


def kernel(
    n_blk,
    n_rep,
    users_ref,
    items_ref,
    hot_ref,
    slot_items_ref,
    slot_values_ref,
    slot_lengths_ref,
    hot_ids_ref,
    hot_count_ref,
    hot_values_ref,
    hot_lengths_ref,
    users_out,
    items_out,
    hot_out,
    eye,
    hot_full,
    codes,
    rating_sum,
    rating_count,
    err,
    user_bf,
    user_t,
    grad_users,
    blocks,
    sent,
    last,
    grads,
    reps_in,
    hot_new,
    *rest,
):
    users_n, rank = users_ref.shape
    stops, slots, _ = slot_items_ref.shape
    width = items_ref.shape[0]
    n_chunks = width // CHUNK
    own_hot = hot_ref.shape[0]
    hot_slots = hot_values_ref.shape[1]
    plan, held_rows = reduce_plan(n_blk, own_hot)
    red_in = rest[: len(plan)]
    (
        block_send,
        block_recv,
        gather_send,
        gather_recv,
        red_send,
        red_recv,
        rep_send,
        rep_recv,
        back_send,
        back_recv,
    ) = rest[len(plan) :]

    b, r = lax.axis_index("blk"), lax.axis_index("rep")
    wrap = r == n_rep - 1
    nxt = (jnp.where(wrap, lax.rem(b + 1, n_blk), b), lax.rem(r + 1, n_rep))
    first = r == 0
    prv = (jnp.where(first, lax.rem(b + n_blk - 1, n_blk), b), lax.rem(r + n_rep - 1, n_rep))

    def bit_of(bit):
        return lax.rem(b // bit, 2)

    def partner(bit):
        return (b + bit * (1 - 2 * bit_of(bit)), r)

    def rep_peer(k):
        return (b, lax.rem(r + k, n_rep))

    barrier = pltpu.get_barrier_semaphore()
    peers = [nxt, prv] + [partner(bit) for bit, _, _ in plan] + [rep_peer(k) for k in range(1, n_rep)]
    for peer in peers:
        pl.semaphore_signal(barrier, inc=1, device_id=peer, device_id_type=MESH)
    pl.semaphore_wait(barrier, len(peers))

    own_at = pl.ds(pl.multiple_of(r * own_hot, own_hot), own_hot)
    hot_full[own_at, :] = hot_ref[...].astype(BF16)
    gathers = []
    for k in range(1, n_rep):
        copy = pltpu.make_async_remote_copy(
            src_ref=hot_full.at[own_at],
            dst_ref=hot_full.at[own_at],
            send_sem=gather_send.at[k - 1],
            recv_sem=gather_recv.at[k - 1],
            device_id=rep_peer(k),
            device_id_type=MESH,
        )
        copy.start()
        gathers.append(copy)

    eye[...] = one_hot(iota(eye.shape, 0) == iota(eye.shape, 1)).astype(BF16)

    def to_blocks(c, carry):
        rows = items_ref[pl.ds(pl.multiple_of(c * CHUNK, CHUNK), CHUNK), :]
        blocks[0, c] = nt(eye[...], rows).astype(BF16)
        return carry

    lax.fori_loop(0, n_chunks, to_blocks, 0)

    lines = 3 * slots
    cols = slots * GROUP
    n_groups = users_n // GROUP

    def expand(t):
        item = slot_items_ref[t]
        live = iota(item.shape, 0) < slot_lengths_ref[pl.ds(t, 1), :]
        place = lax.rem(iota(item.shape, 1), GROUP)
        code = jnp.where(live, (item // LO) * GROUP + place, -1)
        low = lax.rem(item, LO)
        stacked = jnp.concatenate(
            [code.astype(F32).astype(BF16), low.astype(F32).astype(BF16), slot_values_ref[t]], axis=0
        )
        spread = one_hot(iota((lines * GROUP, lines), 0) // GROUP == iota((lines * GROUP, lines), 1))
        wide = nn(spread.astype(BF16), stacked)
        same = lax.rem(iota(wide.shape, 0), GROUP) == lax.rem(iota(wide.shape, 1), GROUP)
        wide = jnp.where(same, wide, 0.0).astype(BF16)
        member = one_hot(iota((n_groups, users_n), 1) // GROUP == iota((n_groups, users_n), 0))
        codes[...] = nt(member.astype(BF16), wide)

        def eight(i, carry):
            packed = codes[pl.ds(pl.multiple_of(i * 8, 8), 8), :]
            levels = iota((LO, cols), 0).astype(F32)
            for j in range(8):
                line = packed[j : j + 1, :]
                left = one_hot(levels == line[:, :cols]).astype(BF16)
                hit = levels == line[:, cols : 2 * cols]
                right = jnp.concatenate(
                    [
                        jnp.where(hit, line[:, 2 * cols :], 0.0).astype(BF16),
                        one_hot(hit).astype(BF16),
                    ],
                    axis=0,
                )
                both = nt(left, right)
                at = pl.ds(pl.multiple_of(i * 8 * GROUP + j * GROUP, GROUP), GROUP)
                for h in range(width // LO):
                    part = both[h * GROUP : (h + 1) * GROUP, :]
                    rating_sum[at, h * LO : (h + 1) * LO] = part[:, :LO]
                    rating_count[at, h * LO : (h + 1) * LO] = part[:, LO:].astype(BF16)
            return carry

        lax.fori_loop(0, n_groups // 8, eight, 0)

    def transpose_users():
        for i in range(users_n // CHUNK):
            rows = slice(i * CHUNK, (i + 1) * CHUNK)
            user_t[:, rows] = nt(eye[...], user_bf[rows, :]).astype(BF16)

    user_bf[...] = users_ref[...].astype(BF16)
    transpose_users()
    expand(0)

    for copy in gathers:
        copy.wait()
    hot_total = hot_full.shape[0]
    hot_t = jnp.concatenate(
        [
            nt(eye[...], hot_full[i * own_hot : (i + 1) * own_hot, :]).astype(BF16)
            for i in range(hot_total // own_hot)
        ],
        axis=1,
    )
    selector = one_hot(iota((hot_total, hot_slots), 0) == hot_ids_ref[...]).astype(BF16)
    hot_slot_t = nn(hot_t, selector).astype(BF16)
    limit = jnp.minimum(hot_lengths_ref[...], hot_count_ref[0]).astype(F32).astype(BF16)
    user_rate = HOT_USER_SCALE / hot_slots
    for i in range(users_n // CHUNK):
        rows = slice(i * CHUNK, (i + 1) * CHUNK)
        predicted = nn(user_bf[rows, :], hot_slot_t)
        bound = nt(eye[...], jnp.broadcast_to(limit[:, rows], (hot_slots, CHUNK)))
        valid = iota(predicted.shape, 1).astype(F32) < bound
        hot_err = jnp.where(valid, hot_values_ref[rows, :].astype(F32) - predicted, 0.0).astype(BF16)
        err[rows, :] = hot_err
        pulled = nt(hot_err, hot_slot_t)
        old = users_ref[rows, :]
        users_out[rows, :] = old + user_rate * (pulled - DECAY_RATE * old)
    slot_grads = nn(user_t[...], err[...])
    dense = jnp.zeros((hot_total, rank), F32)
    for _ in range(3):
        piece = slot_grads.astype(BF16)
        dense = dense + nt(selector, piece)
        slot_grads = slot_grads - piece.astype(F32)
    for i in range(n_rep):
        grads[i] = dense[i * own_hot : (i + 1) * own_hot, :]

    def reduce_steps():
        low = 0
        for i, (bit, held, halve) in enumerate(plan):
            n = held // 2 if halve else held
            away = low + n * (1 - bit_of(bit)) if halve else low
            low = low + n * bit_of(bit) if halve else low
            copy = pltpu.make_async_remote_copy(
                src_ref=grads.at[:, pl.ds(pl.multiple_of(away, 16), n), :],
                dst_ref=red_in[i],
                send_sem=red_send.at[i],
                recv_sem=red_recv.at[i],
                device_id=partner(bit),
                device_id_type=MESH,
            )
            copy.start()
            yield
            copy.wait()
            at = pl.ds(pl.multiple_of(low, 16), n)
            grads[:, at, :] = grads[:, at, :] + red_in[i][...]
        at = pl.ds(pl.multiple_of(low, 16), held_rows)
        copies = []
        for k in range(1, n_rep):
            copy = pltpu.make_async_remote_copy(
                src_ref=grads.at[lax.rem(r + k, n_rep), at, :],
                dst_ref=reps_in.at[k - 1],
                send_sem=rep_send.at[k - 1],
                recv_sem=rep_recv.at[k - 1],
                device_id=rep_peer(k),
                device_id_type=MESH,
            )
            copy.start()
            copies.append(copy)
        yield
        total = grads[r, at, :]
        for k, copy in enumerate(copies):
            copy.wait()
            total = total + reps_in[k]
        old = hot_ref[at, :]
        hot_new[at, :] = old + LEARN_HOT * (total - DECAY_RATE * old)
        for i, (bit, held, halve) in reversed(list(enumerate(plan))):
            if not halve:
                continue
            n = held // 2
            at = pl.ds(pl.multiple_of(low, 16), n)
            copy = pltpu.make_async_remote_copy(
                src_ref=hot_new.at[at],
                dst_ref=hot_new.at[at],
                send_sem=back_send.at[i],
                recv_sem=back_recv.at[i],
                device_id=partner(bit),
                device_id_type=MESH,
            )
            copy.start()
            yield
            copy.wait()
            low = low - n * bit_of(bit)

    steps = reduce_steps()

    def move(t, c):
        at = pl.ds(pl.multiple_of(c * CHUNK, CHUNK), CHUNK)
        return pltpu.make_async_remote_copy(
            src_ref=sent.at[t, c],
            dst_ref=last.at[at] if t == stops - 1 else blocks.at[t + 1, c],
            send_sem=block_send.at[t, c],
            recv_sem=block_recv.at[t, c],
            device_id=nxt,
            device_id_type=MESH,
        )

    def chunk(t, c, carry):
        if t > 0:
            move(t - 1, c).wait_recv()
        block = blocks[t, c]
        lanes = pl.ds(pl.multiple_of(c * CHUNK, CHUNK), CHUNK)
        for i in range(users_n // CHUNK):
            rows = slice(i * CHUNK, (i + 1) * CHUNK)
            predicted = nn(user_bf[rows, :], block)
            errors = rating_sum[rows, lanes] - rating_count[rows, lanes].astype(F32) * predicted
            errors = errors.astype(BF16)
            err[rows, :] = errors
            grad_users[rows, :] += nt(errors, block)
        grad_items = nn(user_t[...], err[...])
        held = block.astype(F32)
        new = (held + LEARN_RATE * (grad_items - DECAY_RATE * held)).astype(BF16)
        if t == stops - 1:
            new = nt(eye[...], new).astype(BF16)
        sent[t, c] = new
        move(t, c).start()
        return carry

    for t in range(stops):
        user_bf[...] = users_out[...].astype(BF16)
        transpose_users()
        grad_users[...] = jnp.zeros_like(grad_users)
        if t > 0:
            expand(t)
            next(steps, None)
        half = n_chunks // 2
        lax.fori_loop(0, half, functools.partial(chunk, t), 0)
        next(steps, None)
        lax.fori_loop(half, n_chunks, functools.partial(chunk, t), 0)
        next(steps, None)
        old = users_out[...]
        users_out[...] = old + LEARN_RATE * (grad_users[...] - DECAY_RATE * old)

    for _ in steps:
        pass
    hot_out[...] = hot_new[...]

    def finish(c, carry):
        move(stops - 1, c).wait_recv()
        at = pl.ds(pl.multiple_of(c * CHUNK, CHUNK), CHUNK)
        items_out[at, :] = last[at, :]
        return carry

    lax.fori_loop(0, n_chunks, finish, 0)
    for t in range(stops):

        def drain(c, carry, t=t):
            move(t, c).wait_send()
            return carry

        lax.fori_loop(0, n_chunks, drain, 0)


def body(
    n_blk,
    n_rep,
    users,
    items,
    hot_factors,
    slot_items,
    slot_values,
    slot_lengths,
    hot_ids,
    hot_count,
    hot_values,
    hot_lengths,
):
    users_n, rank = users.shape
    width = items.shape[0]
    stops, slots, _ = slot_items.shape
    own_hot = hot_factors.shape[0]
    n_chunks = width // CHUNK
    plan, held_rows = reduce_plan(n_blk, own_hot)
    dma = pltpu.SemaphoreType.DMA
    vmem = pl.BlockSpec(memory_space=pltpu.VMEM)
    specs = [vmem] * 10
    specs[7] = pl.BlockSpec(memory_space=pltpu.SMEM)
    scratch = [
        pltpu.VMEM((CHUNK, CHUNK), BF16),
        pltpu.VMEM((n_rep * own_hot, rank), BF16),
        pltpu.VMEM((users_n // GROUP, 3 * slots * GROUP), F32),
        pltpu.VMEM((users_n, width), F32),
        pltpu.VMEM((users_n, width), BF16),
        pltpu.VMEM((users_n, CHUNK), BF16),
        pltpu.VMEM((users_n, rank), BF16),
        pltpu.VMEM((rank, users_n), BF16),
        pltpu.VMEM((users_n, rank), F32),
        pltpu.VMEM((stops, n_chunks, rank, CHUNK), BF16),
        pltpu.VMEM((stops, n_chunks, rank, CHUNK), BF16),
        pltpu.VMEM((width, rank), BF16),
        pltpu.VMEM((n_rep, own_hot, rank), F32),
        pltpu.VMEM((max(n_rep - 1, 1), held_rows, rank), F32),
        pltpu.VMEM((own_hot, rank), F32),
    ]
    for _, held, halve in plan:
        scratch.append(pltpu.VMEM((n_rep, held // 2 if halve else held, rank), F32))
    bits = max(len(plan), 1)
    others = max(n_rep - 1, 1)
    scratch += [
        dma((stops, n_chunks)),
        dma((stops, n_chunks)),
        dma((others,)),
        dma((others,)),
        dma((bits,)),
        dma((bits,)),
        dma((others,)),
        dma((others,)),
        dma((bits,)),
        dma((bits,)),
    ]
    return tuple(
        pl.pallas_call(
            functools.partial(kernel, n_blk, n_rep),
            out_shape=(
                jax.ShapeDtypeStruct(users.shape, F32),
                jax.ShapeDtypeStruct(items.shape, BF16),
                jax.ShapeDtypeStruct(hot_factors.shape, F32),
            ),
            in_specs=specs,
            out_specs=(vmem, vmem, vmem),
            scratch_shapes=scratch,
            compiler_params=pltpu.CompilerParams(
                collective_id=0, has_side_effects=True, vmem_limit_bytes=48 * 2**20
            ),
        )(
            users,
            items,
            hot_factors,
            slot_items,
            slot_values,
            slot_lengths,
            hot_ids.reshape(1, -1),
            hot_count,
            hot_values,
            hot_lengths.reshape(1, -1),
        )
    )


def solution(mesh):
    return jax.shard_map(
        functools.partial(body, mesh.shape["blk"], mesh.shape["rep"]),
        mesh=mesh,
        in_specs=(
            P(("blk", "rep"), None),
            P(("blk", "rep"), None),
            P("rep", None),
            P(None, None, ("blk", "rep")),
            P(None, None, ("blk", "rep")),
            P(None, ("blk", "rep")),
            P(("blk", "rep")),
            P(("blk", "rep")),
            P(("blk", "rep"), None),
            P(("blk", "rep")),
        ),
        out_specs=(P(("blk", "rep"), None), P(("blk", "rep"), None), P("rep", None)),
        check_vma=False,
    )
```

```python
import functools

import jax
import jax.numpy as jnp
from jax import lax
from jax.experimental import pallas as pl
from jax.experimental.pallas import tpu as pltpu
from jax.sharding import PartitionSpec as P

LEARN_RATE = 0.03
DECAY_RATE = 0.02
LEARN_HOT = 0.005
HOT_USER_SCALE = 1.6

F32 = jnp.float32
BF16 = jnp.bfloat16
MESH = pl.DeviceIdType.MESH
GROUP = 16
LO = 128
CHUNK = 256


def nn(a, b):
    return lax.dot_general(a, b, (((1,), (0,)), ((), ())), preferred_element_type=F32)


def nt(a, b):
    return lax.dot_general(a, b, (((1,), (1,)), ((), ())), preferred_element_type=F32)


def iota(shape, dim):
    return lax.broadcasted_iota(jnp.int32, shape, dim)


def one_hot(mask):
    return jnp.where(mask, 1.0, 0.0).astype(F32)


def reduce_plan(n_blk, rows):
    plan, held, bit = [], rows, 1
    while bit < n_blk:
        halve = held >= 32
        plan.append((bit, held, halve))
        held = held // 2 if halve else held
        bit *= 2
    return plan, held


def kernel(
    n_blk,
    n_rep,
    users_hbm,
    items_hbm,
    hot_hbm,
    slot_items_hbm,
    slot_values_hbm,
    slot_lengths_hbm,
    hot_ids_hbm,
    hot_count_ref,
    hot_values_hbm,
    hot_lengths_hbm,
    users_out,
    items_out,
    hot_out,
    eye,
    hot_full,
    codes,
    rating_sum,
    rating_count,
    err,
    user_bf,
    user_t,
    grad_users,
    blocks,
    sent,
    last,
    grads,
    reps_in,
    hot_new,
    users_ref,
    items_ref,
    hot_ref,
    slot_items_ref,
    slot_values_ref,
    slot_lengths_ref,
    hot_ids_ref,
    hot_values_ref,
    hot_lengths_ref,
    hot_err_ref,
    user_t_hot,
    load_sem,
    *rest,
):
    users_n, rank = users_ref.shape
    stops, slots, _ = slot_items_ref.shape
    width = items_ref.shape[0]
    n_chunks = width // CHUNK
    own_hot = hot_ref.shape[0]
    hot_slots = hot_values_ref.shape[1]
    plan, held_rows = reduce_plan(n_blk, own_hot)
    red_in = rest[: len(plan)]
    (
        block_send,
        block_recv,
        gather_send,
        gather_recv,
        red_send,
        red_recv,
        rep_send,
        rep_recv,
        back_send,
        back_recv,
    ) = rest[len(plan) :]

    def load(k, source, target):
        return pltpu.make_async_copy(source, target, load_sem.at[k])

    loads = {
        "hot": load(0, hot_hbm, hot_ref),
        "slot_items": load(1, slot_items_hbm, slot_items_ref),
        "slot_values": load(2, slot_values_hbm, slot_values_ref),
        "slot_lengths": load(3, slot_lengths_hbm, slot_lengths_ref),
        "users": load(4, users_hbm, users_ref),
        "items": load(5, items_hbm, items_ref),
        "hot_values": load(6, hot_values_hbm, hot_values_ref),
        "hot_ids": load(7, hot_ids_hbm, hot_ids_ref),
        "hot_lengths": load(8, hot_lengths_hbm, hot_lengths_ref),
    }
    for copy in loads.values():
        copy.start()

    b, r = lax.axis_index("blk"), lax.axis_index("rep")
    wrap = r == n_rep - 1
    nxt = (jnp.where(wrap, lax.rem(b + 1, n_blk), b), lax.rem(r + 1, n_rep))
    first = r == 0
    prv = (jnp.where(first, lax.rem(b + n_blk - 1, n_blk), b), lax.rem(r + n_rep - 1, n_rep))

    def bit_of(bit):
        return lax.rem(b // bit, 2)

    def partner(bit):
        return (b + bit * (1 - 2 * bit_of(bit)), r)

    def rep_peer(k):
        return (b, lax.rem(r + k, n_rep))

    barrier = pltpu.get_barrier_semaphore()
    peers = [nxt, prv] + [partner(bit) for bit, _, _ in plan] + [rep_peer(k) for k in range(1, n_rep)]
    for peer in peers:
        pl.semaphore_signal(barrier, inc=1, device_id=peer, device_id_type=MESH)
    pl.semaphore_wait(barrier, len(peers))

    own_at = pl.ds(pl.multiple_of(r * own_hot, own_hot), own_hot)
    loads["hot"].wait()
    hot_full[own_at, :] = hot_ref[...].astype(BF16)
    gathers = []
    for k in range(1, n_rep):
        copy = pltpu.make_async_remote_copy(
            src_ref=hot_full.at[own_at],
            dst_ref=hot_full.at[own_at],
            send_sem=gather_send.at[k - 1],
            recv_sem=gather_recv.at[k - 1],
            device_id=rep_peer(k),
            device_id_type=MESH,
        )
        copy.start()
        gathers.append(copy)

    eye[...] = one_hot(iota(eye.shape, 0) == iota(eye.shape, 1)).astype(BF16)

    lines = 3 * slots
    cols = slots * GROUP
    n_groups = users_n // GROUP

    def expand(t):
        item = slot_items_ref[t]
        live = iota(item.shape, 0) < slot_lengths_ref[pl.ds(t, 1), :]
        place = lax.rem(iota(item.shape, 1), GROUP)
        code = jnp.where(live, (item // LO) * GROUP + place, -1)
        low = lax.rem(item, LO)
        stacked = jnp.concatenate(
            [code.astype(F32).astype(BF16), low.astype(F32).astype(BF16), slot_values_ref[t]], axis=0
        )
        spread = one_hot(iota((lines * GROUP, lines), 0) // GROUP == iota((lines * GROUP, lines), 1))
        wide = nn(spread.astype(BF16), stacked)
        same = lax.rem(iota(wide.shape, 0), GROUP) == lax.rem(iota(wide.shape, 1), GROUP)
        wide = jnp.where(same, wide, 0.0).astype(BF16)
        member = one_hot(iota((n_groups, users_n), 1) // GROUP == iota((n_groups, users_n), 0))
        codes[...] = nt(member.astype(BF16), wide)

        def eight(i, carry):
            packed = codes[pl.ds(pl.multiple_of(i * 8, 8), 8), :]
            levels = iota((LO, cols), 0).astype(F32)
            for j in range(8):
                line = packed[j : j + 1, :]
                left = one_hot(levels == line[:, :cols]).astype(BF16)
                hit = levels == line[:, cols : 2 * cols]
                right = jnp.concatenate(
                    [
                        jnp.where(hit, line[:, 2 * cols :], 0.0).astype(BF16),
                        one_hot(hit).astype(BF16),
                    ],
                    axis=0,
                )
                both = nt(left, right)
                at = pl.ds(pl.multiple_of(i * 8 * GROUP + j * GROUP, GROUP), GROUP)
                for h in range(width // LO):
                    part = both[h * GROUP : (h + 1) * GROUP, :]
                    rating_sum[at, h * LO : (h + 1) * LO] = part[:, :LO]
                    rating_count[at, h * LO : (h + 1) * LO] = part[:, LO:].astype(BF16)
            return carry

        lax.fori_loop(0, n_groups // 8, eight, 0)

    def transpose_users(target):
        for i in range(users_n // CHUNK):
            rows = slice(i * CHUNK, (i + 1) * CHUNK)
            target[:, rows] = nt(eye[...], user_bf[rows, :]).astype(BF16)

    for name in ("slot_items", "slot_values", "slot_lengths"):
        loads[name].wait()
    expand(0)
    for name in ("users", "items", "hot_values", "hot_ids", "hot_lengths"):
        loads[name].wait()
    user_bf[...] = users_ref[...].astype(BF16)
    transpose_users(user_t_hot)

    def to_blocks(c, carry):
        rows = items_ref[pl.ds(pl.multiple_of(c * CHUNK, CHUNK), CHUNK), :]
        blocks[0, c] = nt(eye[...], rows).astype(BF16)
        return carry

    lax.fori_loop(0, n_chunks, to_blocks, 0)


    for copy in gathers:
        copy.wait()
    hot_total = hot_full.shape[0]
    hot_t = jnp.concatenate(
        [
            nt(eye[...], hot_full[i * own_hot : (i + 1) * own_hot, :]).astype(BF16)
            for i in range(hot_total // own_hot)
        ],
        axis=1,
    )
    selector = one_hot(iota((hot_total, hot_slots), 0) == hot_ids_ref[...]).astype(BF16)
    hot_slot_t = nn(hot_t, selector).astype(BF16)
    limit = jnp.minimum(hot_lengths_ref[...], hot_count_ref[0]).astype(F32).astype(BF16)
    user_rate = HOT_USER_SCALE / hot_slots
    for i in range(users_n // CHUNK):
        rows = slice(i * CHUNK, (i + 1) * CHUNK)
        predicted = nn(user_bf[rows, :], hot_slot_t)
        bound = nt(eye[...], jnp.broadcast_to(limit[:, rows], (hot_slots, CHUNK)))
        valid = iota(predicted.shape, 1).astype(F32) < bound
        hot_err = jnp.where(valid, hot_values_ref[rows, :].astype(F32) - predicted, 0.0).astype(BF16)
        hot_err_ref[rows, :] = hot_err
        pulled = nt(hot_err, hot_slot_t)
        old = users_ref[rows, :]
        users_out[rows, :] = old + user_rate * (pulled - DECAY_RATE * old)

    def hot_grads():
        slot_grads = nn(user_t_hot[...], hot_err_ref[...])
        dense = jnp.zeros((hot_total, rank), F32)
        for _ in range(3):
            piece = slot_grads.astype(BF16)
            dense = dense + nt(selector, piece)
            slot_grads = slot_grads - piece.astype(F32)
        for i in range(n_rep):
            grads[i] = dense[i * own_hot : (i + 1) * own_hot, :]

    def reduce_steps():
        low = 0
        for i, (bit, held, halve) in enumerate(plan):
            n = held // 2 if halve else held
            away = low + n * (1 - bit_of(bit)) if halve else low
            low = low + n * bit_of(bit) if halve else low
            copy = pltpu.make_async_remote_copy(
                src_ref=grads.at[:, pl.ds(pl.multiple_of(away, 16), n), :],
                dst_ref=red_in[i],
                send_sem=red_send.at[i],
                recv_sem=red_recv.at[i],
                device_id=partner(bit),
                device_id_type=MESH,
            )
            copy.start()
            yield
            copy.wait()
            at = pl.ds(pl.multiple_of(low, 16), n)
            grads[:, at, :] = grads[:, at, :] + red_in[i][...]
        at = pl.ds(pl.multiple_of(low, 16), held_rows)
        copies = []
        for k in range(1, n_rep):
            copy = pltpu.make_async_remote_copy(
                src_ref=grads.at[lax.rem(r + k, n_rep), at, :],
                dst_ref=reps_in.at[k - 1],
                send_sem=rep_send.at[k - 1],
                recv_sem=rep_recv.at[k - 1],
                device_id=rep_peer(k),
                device_id_type=MESH,
            )
            copy.start()
            copies.append(copy)
        yield
        total = grads[r, at, :]
        for k, copy in enumerate(copies):
            copy.wait()
            total = total + reps_in[k]
        old = hot_ref[at, :]
        hot_new[at, :] = old + LEARN_HOT * (total - DECAY_RATE * old)
        for i, (bit, held, halve) in reversed(list(enumerate(plan))):
            if not halve:
                continue
            n = held // 2
            at = pl.ds(pl.multiple_of(low, 16), n)
            copy = pltpu.make_async_remote_copy(
                src_ref=hot_new.at[at],
                dst_ref=hot_new.at[at],
                send_sem=back_send.at[i],
                recv_sem=back_recv.at[i],
                device_id=partner(bit),
                device_id_type=MESH,
            )
            copy.start()
            yield
            copy.wait()
            low = low - n * bit_of(bit)

    steps = reduce_steps()

    def move(t, c):
        at = pl.ds(pl.multiple_of(c * CHUNK, CHUNK), CHUNK)
        return pltpu.make_async_remote_copy(
            src_ref=sent.at[t, c],
            dst_ref=last.at[at] if t == stops - 1 else blocks.at[t + 1, c],
            send_sem=block_send.at[t, c],
            recv_sem=block_recv.at[t, c],
            device_id=nxt,
            device_id_type=MESH,
        )

    def chunk(t, c, carry):
        if t > 0:
            move(t - 1, c).wait_recv()
        block = blocks[t, c]
        lanes = pl.ds(pl.multiple_of(c * CHUNK, CHUNK), CHUNK)
        for i in range(users_n // CHUNK):
            rows = slice(i * CHUNK, (i + 1) * CHUNK)
            predicted = nn(user_bf[rows, :], block)
            errors = rating_sum[rows, lanes] - rating_count[rows, lanes].astype(F32) * predicted
            errors = errors.astype(BF16)
            err[rows, :] = errors
            grad_users[rows, :] += nt(errors, block)
        grad_items = nn(user_t[...], err[...])
        held = block.astype(F32)
        new = (held + LEARN_RATE * (grad_items - DECAY_RATE * held)).astype(BF16)
        if t == stops - 1:
            new = nt(eye[...], new).astype(BF16)
        sent[t, c] = new
        move(t, c).start()
        return carry

    for t in range(stops):
        user_bf[...] = users_out[...].astype(BF16)
        transpose_users(user_t)
        grad_users[...] = jnp.zeros_like(grad_users)
        if t > 0:
            expand(t)
            next(steps, None)
        half = n_chunks // 2
        lax.fori_loop(0, half, functools.partial(chunk, t), 0)
        if t == 0:
            hot_grads()
        next(steps, None)
        lax.fori_loop(half, n_chunks, functools.partial(chunk, t), 0)
        next(steps, None)
        old = users_out[...]
        users_out[...] = old + LEARN_RATE * (grad_users[...] - DECAY_RATE * old)

    for _ in steps:
        pass
    hot_out[...] = hot_new[...]

    def finish(c, carry):
        move(stops - 1, c).wait_recv()
        at = pl.ds(pl.multiple_of(c * CHUNK, CHUNK), CHUNK)
        items_out[at, :] = last[at, :]
        return carry

    lax.fori_loop(0, n_chunks, finish, 0)
    for t in range(stops):

        def drain(c, carry, t=t):
            move(t, c).wait_send()
            return carry

        lax.fori_loop(0, n_chunks, drain, 0)


def body(
    n_blk,
    n_rep,
    users,
    items,
    hot_factors,
    slot_items,
    slot_values,
    slot_lengths,
    hot_ids,
    hot_count,
    hot_values,
    hot_lengths,
):
    users_n, rank = users.shape
    width = items.shape[0]
    stops, slots, _ = slot_items.shape
    own_hot = hot_factors.shape[0]
    n_chunks = width // CHUNK
    plan, held_rows = reduce_plan(n_blk, own_hot)
    dma = pltpu.SemaphoreType.DMA
    vmem = pl.BlockSpec(memory_space=pltpu.VMEM)
    specs = [pl.BlockSpec(memory_space=pltpu.HBM)] * 10
    specs[7] = pl.BlockSpec(memory_space=pltpu.SMEM)
    scratch = [
        pltpu.VMEM((CHUNK, CHUNK), BF16),
        pltpu.VMEM((n_rep * own_hot, rank), BF16),
        pltpu.VMEM((users_n // GROUP, 3 * slots * GROUP), F32),
        pltpu.VMEM((users_n, width), F32),
        pltpu.VMEM((users_n, width), BF16),
        pltpu.VMEM((users_n, CHUNK), BF16),
        pltpu.VMEM((users_n, rank), BF16),
        pltpu.VMEM((rank, users_n), BF16),
        pltpu.VMEM((users_n, rank), F32),
        pltpu.VMEM((stops, n_chunks, rank, CHUNK), BF16),
        pltpu.VMEM((stops, n_chunks, rank, CHUNK), BF16),
        pltpu.VMEM((width, rank), BF16),
        pltpu.VMEM((n_rep, own_hot, rank), F32),
        pltpu.VMEM((max(n_rep - 1, 1), held_rows, rank), F32),
        pltpu.VMEM((own_hot, rank), F32),
        pltpu.VMEM(users.shape, F32),
        pltpu.VMEM(items.shape, BF16),
        pltpu.VMEM(hot_factors.shape, F32),
        pltpu.VMEM(slot_items.shape, jnp.int32),
        pltpu.VMEM(slot_values.shape, BF16),
        pltpu.VMEM(slot_lengths.shape, jnp.int32),
        pltpu.VMEM((1, hot_ids.shape[0]), jnp.int32),
        pltpu.VMEM(hot_values.shape, BF16),
        pltpu.VMEM((1, users_n), jnp.int32),
        pltpu.VMEM(hot_values.shape, BF16),
        pltpu.VMEM((rank, users_n), BF16),
        dma((9,)),
    ]
    for _, held, halve in plan:
        scratch.append(pltpu.VMEM((n_rep, held // 2 if halve else held, rank), F32))
    bits = max(len(plan), 1)
    others = max(n_rep - 1, 1)
    scratch += [
        dma((stops, n_chunks)),
        dma((stops, n_chunks)),
        dma((others,)),
        dma((others,)),
        dma((bits,)),
        dma((bits,)),
        dma((others,)),
        dma((others,)),
        dma((bits,)),
        dma((bits,)),
    ]
    return tuple(
        pl.pallas_call(
            functools.partial(kernel, n_blk, n_rep),
            out_shape=(
                jax.ShapeDtypeStruct(users.shape, F32),
                jax.ShapeDtypeStruct(items.shape, BF16),
                jax.ShapeDtypeStruct(hot_factors.shape, F32),
            ),
            in_specs=specs,
            out_specs=(vmem, vmem, vmem),
            scratch_shapes=scratch,
            compiler_params=pltpu.CompilerParams(
                collective_id=0, has_side_effects=True, vmem_limit_bytes=63 * 2**20
            ),
        )(
            users,
            items,
            hot_factors,
            slot_items,
            slot_values,
            slot_lengths,
            hot_ids.reshape(1, -1),
            hot_count,
            hot_values,
            hot_lengths.reshape(1, -1),
        )
    )


def solution(mesh):
    return jax.shard_map(
        functools.partial(body, mesh.shape["blk"], mesh.shape["rep"]),
        mesh=mesh,
        in_specs=(
            P(("blk", "rep"), None),
            P(("blk", "rep"), None),
            P("rep", None),
            P(None, None, ("blk", "rep")),
            P(None, None, ("blk", "rep")),
            P(None, ("blk", "rep")),
            P(("blk", "rep")),
            P(("blk", "rep")),
            P(("blk", "rep"), None),
            P(("blk", "rep")),
        ),
        out_specs=(P(("blk", "rep"), None), P(("blk", "rep"), None), P("rep", None)),
        check_vma=False,
    )
```

```python
import functools

import jax
import jax.numpy as jnp
from jax import lax
from jax.experimental import pallas as pl
from jax.experimental.pallas import tpu as pltpu
from jax.sharding import PartitionSpec as P

LEARN_RATE = 0.03
DECAY_RATE = 0.02
LEARN_HOT = 0.005
HOT_USER_SCALE = 1.6

F32 = jnp.float32
BF16 = jnp.bfloat16
MESH = pl.DeviceIdType.MESH
GROUP = 16
LO = 128
CHUNK = 256


def nn(a, b):
    return lax.dot_general(a, b, (((1,), (0,)), ((), ())), preferred_element_type=F32)


def nt(a, b):
    return lax.dot_general(a, b, (((1,), (1,)), ((), ())), preferred_element_type=F32)


def iota(shape, dim):
    return lax.broadcasted_iota(jnp.int32, shape, dim)


def one_hot(mask):
    return jnp.where(mask, 1.0, 0.0).astype(F32)


def reduce_plan(n_blk, rows):
    plan, held, bit = [], rows, 1
    while bit < n_blk:
        halve = held >= 32
        plan.append((bit, held, halve))
        held = held // 2 if halve else held
        bit *= 2
    return plan, held


def kernel(
    n_blk,
    n_rep,
    users_hbm,
    items_hbm,
    hot_hbm,
    slot_items_hbm,
    slot_values_hbm,
    slot_lengths_hbm,
    hot_ids_hbm,
    hot_count_ref,
    hot_values_hbm,
    hot_lengths_hbm,
    users_out,
    items_out,
    hot_out,
    eye,
    hot_full,
    codes,
    rating_sum,
    rating_count,
    err,
    user_bf,
    user_t,
    grad_users,
    blocks,
    sent,
    last,
    grads,
    reps_in,
    hot_new,
    users_ref,
    items_ref,
    hot_ref,
    slot_items_ref,
    slot_values_ref,
    slot_lengths_ref,
    hot_ids_ref,
    hot_values_ref,
    hot_lengths_ref,
    hot_err_ref,
    user_t_hot,
    load_sem,
    *rest,
):
    users_n, rank = users_ref.shape
    stops, slots, _ = slot_items_ref.shape
    width = items_ref.shape[0]
    n_chunks = width // CHUNK
    own_hot = hot_ref.shape[0]
    hot_slots = hot_values_ref.shape[1]
    plan, held_rows = reduce_plan(n_blk, own_hot)
    red_in = rest[: len(plan)]
    (
        block_send,
        block_recv,
        gather_send,
        gather_recv,
        red_send,
        red_recv,
        rep_send,
        rep_recv,
        back_send,
        back_recv,
    ) = rest[len(plan) :]

    def load(k, source, target):
        return pltpu.make_async_copy(source, target, load_sem.at[k])

    loads = {
        "hot": load(0, hot_hbm, hot_ref),
        "slot_items": load(1, slot_items_hbm, slot_items_ref),
        "slot_values": load(2, slot_values_hbm, slot_values_ref),
        "slot_lengths": load(3, slot_lengths_hbm, slot_lengths_ref),
        "users": load(4, users_hbm, users_ref),
        "items": load(5, items_hbm, items_ref),
        "hot_values": load(6, hot_values_hbm, hot_values_ref),
        "hot_ids": load(7, hot_ids_hbm, hot_ids_ref),
        "hot_lengths": load(8, hot_lengths_hbm, hot_lengths_ref),
    }
    for copy in loads.values():
        copy.start()

    b, r = lax.axis_index("blk"), lax.axis_index("rep")
    wrap = r == n_rep - 1
    nxt = (jnp.where(wrap, lax.rem(b + 1, n_blk), b), lax.rem(r + 1, n_rep))
    first = r == 0
    prv = (jnp.where(first, lax.rem(b + n_blk - 1, n_blk), b), lax.rem(r + n_rep - 1, n_rep))

    def bit_of(bit):
        return lax.rem(b // bit, 2)

    def partner(bit):
        return (b + bit * (1 - 2 * bit_of(bit)), r)

    def rep_peer(k):
        return (b, lax.rem(r + k, n_rep))

    barrier = pltpu.get_barrier_semaphore()
    peers = [nxt, prv] + [partner(bit) for bit, _, _ in plan] + [rep_peer(k) for k in range(1, n_rep)]
    for peer in peers:
        pl.semaphore_signal(barrier, inc=1, device_id=peer, device_id_type=MESH)
    pl.semaphore_wait(barrier, len(peers))

    own_at = pl.ds(pl.multiple_of(r * own_hot, own_hot), own_hot)
    loads["hot"].wait()
    hot_full[own_at, :] = hot_ref[...].astype(BF16)
    gathers = []
    for k in range(1, n_rep):
        copy = pltpu.make_async_remote_copy(
            src_ref=hot_full.at[own_at],
            dst_ref=hot_full.at[own_at],
            send_sem=gather_send.at[k - 1],
            recv_sem=gather_recv.at[k - 1],
            device_id=rep_peer(k),
            device_id_type=MESH,
        )
        copy.start()
        gathers.append(copy)

    eye[...] = one_hot(iota(eye.shape, 0) == iota(eye.shape, 1)).astype(BF16)

    lines = 3 * slots
    cols = slots * GROUP
    n_groups = users_n // GROUP

    def expand(t):
        item = slot_items_ref[t]
        live = iota(item.shape, 0) < slot_lengths_ref[pl.ds(t, 1), :]
        place = lax.rem(iota(item.shape, 1), GROUP)
        code = jnp.where(live, (item // LO) * GROUP + place, -1)
        low = lax.rem(item, LO)
        stacked = jnp.concatenate(
            [code.astype(F32).astype(BF16), low.astype(F32).astype(BF16), slot_values_ref[t]], axis=0
        )
        spread = one_hot(iota((lines * GROUP, lines), 0) // GROUP == iota((lines * GROUP, lines), 1))
        wide = nn(spread.astype(BF16), stacked)
        same = lax.rem(iota(wide.shape, 0), GROUP) == lax.rem(iota(wide.shape, 1), GROUP)
        wide = jnp.where(same, wide, 0.0).astype(BF16)
        member = one_hot(iota((n_groups, users_n), 1) // GROUP == iota((n_groups, users_n), 0))
        codes[...] = nt(member.astype(BF16), wide)

        def eight(i, carry):
            packed = codes[pl.ds(pl.multiple_of(i * 8, 8), 8), :]
            levels = iota((LO, cols), 0).astype(F32)
            for j in range(8):
                line = packed[j : j + 1, :]
                left = one_hot(levels == line[:, :cols]).astype(BF16)
                hit = levels == line[:, cols : 2 * cols]
                right = jnp.concatenate(
                    [
                        jnp.where(hit, line[:, 2 * cols :], 0.0).astype(BF16),
                        one_hot(hit).astype(BF16),
                    ],
                    axis=0,
                )
                both = nt(left, right)
                at = pl.ds(pl.multiple_of(i * 8 * GROUP + j * GROUP, GROUP), GROUP)
                for h in range(width // LO):
                    part = both[h * GROUP : (h + 1) * GROUP, :]
                    rating_sum[at, h * LO : (h + 1) * LO] = part[:, :LO]
                    rating_count[at, h * LO : (h + 1) * LO] = part[:, LO:].astype(BF16)
            return carry

        lax.fori_loop(0, n_groups // 8, eight, 0)

    def transpose_users(target):
        for i in range(users_n // CHUNK):
            rows = slice(i * CHUNK, (i + 1) * CHUNK)
            target[:, rows] = nt(eye[...], user_bf[rows, :]).astype(BF16)

    for name in ("slot_items", "slot_values", "slot_lengths"):
        loads[name].wait()
    expand(0)
    for name in ("users", "items", "hot_values", "hot_ids", "hot_lengths"):
        loads[name].wait()
    user_bf[...] = users_ref[...].astype(BF16)
    transpose_users(user_t_hot)

    def to_blocks(c, carry):
        rows = items_ref[pl.ds(pl.multiple_of(c * CHUNK, CHUNK), CHUNK), :]
        blocks[0, c] = nt(eye[...], rows).astype(BF16)
        return carry

    lax.fori_loop(0, n_chunks, to_blocks, 0)


    for copy in gathers:
        copy.wait()
    hot_total = hot_full.shape[0]
    hot_t = jnp.concatenate(
        [
            nt(eye[...], hot_full[i * own_hot : (i + 1) * own_hot, :]).astype(BF16)
            for i in range(hot_total // own_hot)
        ],
        axis=1,
    )
    selector = one_hot(iota((hot_total, hot_slots), 0) == hot_ids_ref[...]).astype(BF16)
    hot_slot_t = nn(hot_t, selector).astype(BF16)
    limit = jnp.minimum(hot_lengths_ref[...], hot_count_ref[0]).astype(F32).astype(BF16)
    user_rate = HOT_USER_SCALE / hot_slots
    for i in range(users_n // CHUNK):
        rows = slice(i * CHUNK, (i + 1) * CHUNK)
        predicted = nn(user_bf[rows, :], hot_slot_t)
        bound = nt(eye[...], jnp.broadcast_to(limit[:, rows], (hot_slots, CHUNK)))
        valid = iota(predicted.shape, 1).astype(F32) < bound
        hot_err = jnp.where(valid, hot_values_ref[rows, :].astype(F32) - predicted, 0.0).astype(BF16)
        hot_err_ref[rows, :] = hot_err
        pulled = nt(hot_err, hot_slot_t)
        old = users_ref[rows, :]
        users_out[rows, :] = old + user_rate * (pulled - DECAY_RATE * old)

    def hot_grads():
        slot_grads = nn(user_t_hot[...], hot_err_ref[...])
        dense = jnp.zeros((hot_total, rank), F32)
        for _ in range(3):
            piece = slot_grads.astype(BF16)
            dense = dense + nt(selector, piece)
            slot_grads = slot_grads - piece.astype(F32)
        for i in range(n_rep):
            grads[i] = dense[i * own_hot : (i + 1) * own_hot, :]

    def reduce_steps():
        low = 0
        for i, (bit, held, halve) in enumerate(plan):
            n = held // 2 if halve else held
            away = low + n * (1 - bit_of(bit)) if halve else low
            low = low + n * bit_of(bit) if halve else low
            copy = pltpu.make_async_remote_copy(
                src_ref=grads.at[:, pl.ds(pl.multiple_of(away, 16), n), :],
                dst_ref=red_in[i],
                send_sem=red_send.at[i],
                recv_sem=red_recv.at[i],
                device_id=partner(bit),
                device_id_type=MESH,
            )
            copy.start()
            yield
            copy.wait()
            at = pl.ds(pl.multiple_of(low, 16), n)
            grads[:, at, :] = grads[:, at, :] + red_in[i][...]
        at = pl.ds(pl.multiple_of(low, 16), held_rows)
        copies = []
        for k in range(1, n_rep):
            copy = pltpu.make_async_remote_copy(
                src_ref=grads.at[lax.rem(r + k, n_rep), at, :],
                dst_ref=reps_in.at[k - 1],
                send_sem=rep_send.at[k - 1],
                recv_sem=rep_recv.at[k - 1],
                device_id=rep_peer(k),
                device_id_type=MESH,
            )
            copy.start()
            copies.append(copy)
        yield
        total = grads[r, at, :]
        for k, copy in enumerate(copies):
            copy.wait()
            total = total + reps_in[k]
        old = hot_ref[at, :]
        hot_new[at, :] = old + LEARN_HOT * (total - DECAY_RATE * old)
        for i, (bit, held, halve) in reversed(list(enumerate(plan))):
            if not halve:
                continue
            n = held // 2
            at = pl.ds(pl.multiple_of(low, 16), n)
            copy = pltpu.make_async_remote_copy(
                src_ref=hot_new.at[at],
                dst_ref=hot_new.at[at],
                send_sem=back_send.at[i],
                recv_sem=back_recv.at[i],
                device_id=partner(bit),
                device_id_type=MESH,
            )
            copy.start()
            yield
            copy.wait()
            low = low - n * bit_of(bit)

    steps = reduce_steps()

    def move(t, c):
        at = pl.ds(pl.multiple_of(c * CHUNK, CHUNK), CHUNK)
        return pltpu.make_async_remote_copy(
            src_ref=sent.at[t, c],
            dst_ref=last.at[at] if t == stops - 1 else blocks.at[t + 1, c],
            send_sem=block_send.at[t, c],
            recv_sem=block_recv.at[t, c],
            device_id=nxt,
            device_id_type=MESH,
        )

    def chunk(t, c, carry):
        if t > 0:
            move(t - 1, c).wait_recv()
        block = blocks[t, c]
        lanes = pl.ds(pl.multiple_of(c * CHUNK, CHUNK), CHUNK)
        for i in range(users_n // CHUNK):
            rows = slice(i * CHUNK, (i + 1) * CHUNK)
            predicted = nn(user_bf[rows, :], block)
            errors = rating_sum[rows, lanes] - rating_count[rows, lanes].astype(F32) * predicted
            errors = errors.astype(BF16)
            err[rows, :] = errors
            grad_users[rows, :] += nt(errors, block)
        grad_items = nn(user_t[...], err[...])
        held = block.astype(F32)
        new = (held + LEARN_RATE * (grad_items - DECAY_RATE * held)).astype(BF16)
        if t == stops - 1:
            new = nt(eye[...], new).astype(BF16)
        sent[t, c] = new
        move(t, c).start()
        return carry

    for t in range(stops):
        user_bf[...] = users_out[...].astype(BF16)
        transpose_users(user_t)
        grad_users[...] = jnp.zeros_like(grad_users)
        if t > 0:
            expand(t)
            next(steps, None)
        half = n_chunks // 2
        lax.fori_loop(0, half, functools.partial(chunk, t), 0)
        if t == 0:
            hot_grads()
        next(steps, None)
        lax.fori_loop(half, n_chunks, functools.partial(chunk, t), 0)
        if t == 0:
            next(steps, None)
        old = users_out[...]
        users_out[...] = old + LEARN_RATE * (grad_users[...] - DECAY_RATE * old)

    for _ in steps:
        pass
    hot_out[...] = hot_new[...]

    def finish(c, carry):
        move(stops - 1, c).wait_recv()
        at = pl.ds(pl.multiple_of(c * CHUNK, CHUNK), CHUNK)
        items_out[at, :] = last[at, :]
        return carry

    lax.fori_loop(0, n_chunks, finish, 0)
    for t in range(stops):

        def drain(c, carry, t=t):
            move(t, c).wait_send()
            return carry

        lax.fori_loop(0, n_chunks, drain, 0)


def write_out(*refs):
    *refs, sem = refs
    copies = [pltpu.make_async_copy(refs[i], refs[i + 3], sem.at[i]) for i in range(3)]
    for copy in copies:
        copy.start()
    for copy in copies:
        copy.wait()


def body(
    n_blk,
    n_rep,
    users,
    items,
    hot_factors,
    slot_items,
    slot_values,
    slot_lengths,
    hot_ids,
    hot_count,
    hot_values,
    hot_lengths,
):
    users_n, rank = users.shape
    width = items.shape[0]
    stops, slots, _ = slot_items.shape
    own_hot = hot_factors.shape[0]
    n_chunks = width // CHUNK
    plan, held_rows = reduce_plan(n_blk, own_hot)
    dma = pltpu.SemaphoreType.DMA
    vmem = pl.BlockSpec(memory_space=pltpu.VMEM)
    specs = [pl.BlockSpec(memory_space=pltpu.HBM)] * 10
    specs[7] = pl.BlockSpec(memory_space=pltpu.SMEM)
    scratch = [
        pltpu.VMEM((CHUNK, CHUNK), BF16),
        pltpu.VMEM((n_rep * own_hot, rank), BF16),
        pltpu.VMEM((users_n // GROUP, 3 * slots * GROUP), F32),
        pltpu.VMEM((users_n, width), F32),
        pltpu.VMEM((users_n, width), BF16),
        pltpu.VMEM((users_n, CHUNK), BF16),
        pltpu.VMEM((users_n, rank), BF16),
        pltpu.VMEM((rank, users_n), BF16),
        pltpu.VMEM((users_n, rank), F32),
        pltpu.VMEM((stops, n_chunks, rank, CHUNK), BF16),
        pltpu.VMEM((stops, n_chunks, rank, CHUNK), BF16),
        pltpu.VMEM((width, rank), BF16),
        pltpu.VMEM((n_rep, own_hot, rank), F32),
        pltpu.VMEM((max(n_rep - 1, 1), held_rows, rank), F32),
        pltpu.VMEM((own_hot, rank), F32),
        pltpu.VMEM(users.shape, F32),
        pltpu.VMEM(items.shape, BF16),
        pltpu.VMEM(hot_factors.shape, F32),
        pltpu.VMEM(slot_items.shape, jnp.int32),
        pltpu.VMEM(slot_values.shape, BF16),
        pltpu.VMEM(slot_lengths.shape, jnp.int32),
        pltpu.VMEM((1, hot_ids.shape[0]), jnp.int32),
        pltpu.VMEM(hot_values.shape, BF16),
        pltpu.VMEM((1, users_n), jnp.int32),
        pltpu.VMEM(hot_values.shape, BF16),
        pltpu.VMEM((rank, users_n), BF16),
        dma((9,)),
    ]
    for _, held, halve in plan:
        scratch.append(pltpu.VMEM((n_rep, held // 2 if halve else held, rank), F32))
    bits = max(len(plan), 1)
    others = max(n_rep - 1, 1)
    scratch += [
        dma((stops, n_chunks)),
        dma((stops, n_chunks)),
        dma((others,)),
        dma((others,)),
        dma((bits,)),
        dma((bits,)),
        dma((others,)),
        dma((others,)),
        dma((bits,)),
        dma((bits,)),
    ]
    outs = tuple(
        pl.pallas_call(
            functools.partial(kernel, n_blk, n_rep),
            out_shape=(
                jax.ShapeDtypeStruct(users.shape, F32),
                jax.ShapeDtypeStruct(items.shape, BF16),
                jax.ShapeDtypeStruct(hot_factors.shape, F32),
            ),
            in_specs=specs,
            out_specs=(vmem, vmem, vmem),
            scratch_shapes=scratch,
            compiler_params=pltpu.CompilerParams(
                collective_id=0, has_side_effects=True, vmem_limit_bytes=63 * 2**20
            ),
        )(
            users,
            items,
            hot_factors,
            slot_items,
            slot_values,
            slot_lengths,
            hot_ids.reshape(1, -1),
            hot_count,
            hot_values,
            hot_lengths.reshape(1, -1),
        )
    )
    hbm = pl.BlockSpec(memory_space=pltpu.HBM)
    return tuple(
        pl.pallas_call(
            write_out,
            out_shape=tuple(jax.ShapeDtypeStruct(x.shape, x.dtype) for x in outs),
            in_specs=[hbm] * 3,
            out_specs=(hbm,) * 3,
            scratch_shapes=[dma((3,))],
        )(*outs)
    )


def solution(mesh):
    return jax.shard_map(
        functools.partial(body, mesh.shape["blk"], mesh.shape["rep"]),
        mesh=mesh,
        in_specs=(
            P(("blk", "rep"), None),
            P(("blk", "rep"), None),
            P("rep", None),
            P(None, None, ("blk", "rep")),
            P(None, None, ("blk", "rep")),
            P(None, ("blk", "rep")),
            P(("blk", "rep")),
            P(("blk", "rep")),
            P(("blk", "rep"), None),
            P(("blk", "rep")),
        ),
        out_specs=(P(("blk", "rep"), None), P(("blk", "rep"), None), P("rep", None)),
        check_vma=False,
    )
```
